512 devices in a mesh: replica: 32 (over z, y_lo), fsdp: 16 (over x, y_hi, core).
Axes of the slice: x: 4, y: 4 (y_hi: 2, y_lo: 2; y = y_hi * 2 + y_lo), z: 16, core: 2. Of those that a mesh axis runs over, the one named last changes fastest.
Arguments:
- tokens: bfloat16 [98304, 8192], P(('replica', 'fsdp')), may hold values from -6 to 6
- master: float32 [8192, 512], P(('fsdp', 'replica')), may hold values from -1 to 1, as said below
- momentum: float32 [8192, 512], P(('fsdp', 'replica')), may hold values from -0.046875 to 0.046875
- trained: bfloat16 [32, 8192, 512], P('replica', 'fsdp'), may hold values from -1 to 1, as said below
Outputs:
- new_master: float32 [8192, 512], P(('fsdp', 'replica'))
- new_momentum: float32 [8192, 512], P(('fsdp', 'replica'))
- refreshed: bfloat16 [8192, 512], P('fsdp')
- keys: float32 [98304, 512], P(('replica', 'fsdp'))
The draws below stay inside these ranges and needn't reach their ends.
Inputs may be any that keep to these rules, and one draw needn't show every extreme that they name: master is a weight matrix of scale about 8192 ** -0.5. Each replica's trained weights are the bfloat16 start weights plus that replica's drift.
All inputs are finite; a program needn't handle non-finite values.
Results may differ from the reference program's by a relative error of at most 0.012.
Values may be sent and summed in bfloat16 or wider, within the bound.
No kernel may reach another device: no remote copies, remote signals or barrier semaphores. Data moves between devices by JAX's collectives and lax.ppermute only.
A program may use at most 64 MiB of HBM per device.

```python
import jax
import jax.numpy as jnp
from jax import lax

D = 8192
KV = 512
REPLICAS = 32
ROWS_OWN = 16
TOKENS = 98304


def base_weights(key):
    values = jnp.clip(jax.random.normal(key, (D, KV), jnp.float32), -5.0, 5.0)
    return values * D ** (-0.5)


def draw_master(key, part):
    return base_weights(key).astype(jnp.float32)


def draw_trained(key, part):
    begin_weights = base_weights(key).astype(jnp.bfloat16).astype(jnp.float32)
    key = jax.random.fold_in(key, 7)
    key_drift, key_shift = jax.random.split(key, 2)
    drift = jnp.clip(jax.random.normal(key_drift, (REPLICAS, D, KV), jnp.float32), -5.0, 5.0)
    row_block = jnp.arange(D, dtype=jnp.int32) // ROWS_OWN % REPLICAS
    shift_value = jax.random.randint(key_shift, (), 0, REPLICAS, jnp.int32)
    replica_ids = jnp.arange(REPLICAS, dtype=jnp.int32)
    paired = row_block[None, :] == (replica_ids[:, None] + shift_value) % REPLICAS
    factor = jnp.where(paired, 6.0, 1.0)[:, :, None]
    values = begin_weights[None] + 0.25 * D ** (-0.5) * drift * factor
    return values.astype(jnp.bfloat16)


def block_levels(key, shape, cuts, least, top_value):
    def one(axis_at, blocks):
        heights = jax.random.uniform(jax.random.fold_in(jax.random.fold_in(key, 6), axis_at), (blocks,), jnp.float32, least / len(cuts), top_value / len(cuts))
        return jnp.repeat(jnp.exp(heights), shape[axis_at] // blocks).reshape((-1,) + (1,) * (len(shape) - axis_at - 1))

    factor_of = one(*cuts[0])
    for cut in cuts[1:]:
        factor_of = factor_of * one(*cut)
    return factor_of


def scatter_about(rng, extent, width, limit, shards=(), held_as=jnp.bfloat16):
    array = width * jax.random.normal(rng, extent, jnp.float32)
    if shards:
        array = array * block_levels(rng, extent, shards, -0.22, 0.18)
    return jnp.clip(array, -limit, limit).astype(held_as)


def setup_inputs(seed: int = 0) -> dict:
    arg_keys = jax.random.split(jax.random.key(seed), 5)
    tokens = scatter_about(arg_keys[0], (TOKENS, D), 1.0, 6.0, ((0, 512),))
    master = draw_master(jax.random.fold_in(arg_keys[4], 71), 0)
    momentum = scatter_about(arg_keys[2], (D, KV), 0.003, 0.046875, ((0, 512),), jnp.float32)
    trained = draw_trained(jax.random.fold_in(arg_keys[4], 71), 0)
    return {"tokens": tokens, "master": master, "momentum": momentum, "trained": trained}


outer_rate = 0.7
decay_factor = 0.9


def reference(tokens, master, momentum, trained):
    def accumulate(running, weights):
        return running + weights.astype(jnp.float32), None

    summed, _ = lax.scan(accumulate, jnp.zeros(master.shape, jnp.float32), trained)
    rounded = lax.optimization_barrier(master.astype(jnp.bfloat16))
    begin_weights = rounded.astype(jnp.float32)
    pseudo = begin_weights - summed / REPLICAS
    new_momentum = decay_factor * momentum + pseudo
    new_master = master - outer_rate * (pseudo + decay_factor * new_momentum)
    refreshed = new_master.astype(jnp.bfloat16)
    keys = jnp.dot(tokens, refreshed, preferred_element_type=jnp.float32)
    return (new_master, new_momentum, refreshed, keys)
```

```python
import jax
import jax.numpy as jnp
from jax import lax
from jax.experimental import pallas as pl
from jax.experimental.pallas import tpu as pltpu
from jax.sharding import Mesh, PartitionSpec as P

outer_rate = 0.7
decay_factor = 0.9


def outer_step(summed, master_rows, momentum_rows, replicas):
    rounded = lax.optimization_barrier(master_rows.astype(jnp.bfloat16))
    begin_weights = rounded.astype(jnp.float32)
    pseudo = begin_weights - summed / replicas
    new_momentum = decay_factor * momentum_rows + pseudo
    new_master = master_rows - outer_rate * (pseudo + decay_factor * new_momentum)
    return (new_master, new_momentum)


def spread(block, axis, n):
    copies = jnp.broadcast_to(block[None], (n,) + block.shape)
    return lax.all_to_all(copies, axis, 0, 0, tiled=True)


def keys_kernel(at, own, other, t0, t1, t2, t3, out, fresh, w, t, o, sem_w, sem_t, sem_o, sem_f):
    x, yh, c = at[0], at[1], at[2]
    nl, nh = own.shape[:2]
    nx = t.shape[0]
    loads = []
    for h in range(nh):
        for l in range(nl):
            for i, (source, core) in enumerate(((own, c), (other, 1 - c))):
                copy = pltpu.make_async_copy(source.at[l, h], w.at[h, core, :, l], sem_w.at[i, h * nl + l])
                copy.start()
                loads.append(copy)
    taken = []
    for d, source in enumerate((t0, t1, t2, t3)):
        copy = pltpu.make_async_copy(source, t.at[d], sem_t.at[d])
        copy.start()
        taken.append(copy)
    for copy in loads:
        copy.wait()
    for l in range(nl):
        pltpu.make_async_copy(w.at[yh, c, :, l], fresh.at[:, l], sem_f.at[l]).start()
    weights = w[...].reshape(t.shape[2], out.shape[2])
    sent = []
    for d in range(nx):
        taken[d].wait()
        o[d] = jnp.dot(t[d], weights, preferred_element_type=jnp.float32).astype(o.dtype)
        copy = pltpu.make_async_copy(o.at[d], out.at[lax.rem(x + nx - d, nx)], sem_o.at[d])
        copy.start()
        sent.append(copy)
    for l in range(nl):
        pltpu.make_async_copy(w.at[yh, c, :, l], fresh.at[:, l], sem_f.at[l]).wait()
    for copy in sent:
        copy.wait()


def multiply(at, own, other, pieces):
    nl, nh, nz, rows, kv = own.shape
    nx = len(pieces)
    tok, part = pieces[0].shape
    hbm = pl.BlockSpec(memory_space=pl.ANY)
    return pl.pallas_call(
        keys_kernel,
        out_shape=(
            jax.ShapeDtypeStruct((nx, tok, kv), jnp.bfloat16),
            jax.ShapeDtypeStruct((nz, nl, rows, kv), jnp.bfloat16),
        ),
        in_specs=[pl.BlockSpec(memory_space=pltpu.SMEM)] + [hbm] * (2 + nx),
        out_specs=(hbm, hbm),
        scratch_shapes=[
            pltpu.VMEM((nh, 2, nz, nl, rows, kv), jnp.bfloat16),
            pltpu.VMEM((nx, tok, part), jnp.bfloat16),
            pltpu.VMEM((nx, tok, kv), jnp.bfloat16),
            pltpu.SemaphoreType.DMA((2, nh * nl)),
            pltpu.SemaphoreType.DMA((nx,)),
            pltpu.SemaphoreType.DMA((nx,)),
            pltpu.SemaphoreType.DMA((nl,)),
        ],
        compiler_params=pltpu.CompilerParams(vmem_limit_bytes=12 * 2**20),
        cost_estimate=pl.CostEstimate(
            flops=2 * nx * tok * part * kv, bytes_accessed=8 * 2**20, transcendentals=0
        ),
    )(at, own, other, *(pltpu.with_memory_space_constraint(p, pltpu.HBM) for p in pieces))


def local(tokens, master, momentum, trained):
    nz, nl, nx, nh, nc = (lax.axis_size(a) for a in ("z", "yl", "x", "yh", "c"))
    rows, kv = master.shape
    tok, depth = tokens.shape
    x, yh, c = lax.axis_index("x"), lax.axis_index("yh"), lax.axis_index("c")
    part = depth // nx

    owned = lax.all_to_all(trained[0].reshape(nz * nl, rows, kv), ("z", "yl"), 0, 0, tiled=True)
    summed = jnp.sum(owned.astype(jnp.float32), axis=0)
    new_master, new_momentum = outer_step(summed, master, momentum, nz * nl)
    fresh = new_master.astype(jnp.bfloat16)

    pieces = []
    for d in range(nx):
        piece = lax.dynamic_slice(tokens, (0, (x + d) % nx * part), (tok, part))
        if d:
            piece = lax.ppermute(piece, "x", [(i, (i + d) % nx) for i in range(nx)])
        pieces.append(piece)
    fresh, pieces[1], pieces[3] = lax.optimization_barrier((fresh, pieces[1], pieces[3]))

    rows_z = spread(fresh, "z", nz)
    rows_z, *pieces = lax.optimization_barrier((rows_z, *pieces))
    rows_y = spread(rows_z, ("yl", "yh"), nl * nh).reshape(nl, nh, nz, rows, kv)
    others = lax.ppermute(rows_y, "c", [(0, 1), (1, 0)])

    share, refreshed = multiply(jnp.stack([x, yh, c]).astype(jnp.int32), rows_y, others, pieces)
    share = lax.all_to_all(share, "x", 0, 0, tiled=True)
    key_values = jnp.sum(share.astype(jnp.float32), axis=0)
    return (new_master, new_momentum, refreshed.reshape(-1, kv), key_values)


def solution(mesh):
    fine = Mesh(mesh.devices.reshape(16, 2, 4, 2, 2), ("z", "yl", "x", "yh", "c"))
    replica, fsdp = ("z", "yl"), ("x", "yh", "c")
    in_specs = (
        P(replica + fsdp, None),
        P(fsdp + replica, None),
        P(fsdp + replica, None),
        P(replica, fsdp, None),
    )
    out_specs = (
        P(fsdp + replica, None),
        P(fsdp + replica, None),
        P(fsdp, None),
        P(replica + fsdp, None),
    )
    return jax.shard_map(local, mesh=fine, in_specs=in_specs, out_specs=out_specs, check_vma=False)
```

```python
import itertools
import math

import jax
import jax.numpy as jnp
from jax import lax
from jax.experimental import pallas as pl
from jax.experimental.pallas import tpu as pltpu
from jax.sharding import Mesh, PartitionSpec as P

outer_rate = 0.7
decay_factor = 0.9


def exchange(blocks, along, across, turn):
    n = math.prod(lax.axis_size(a) for a in along)
    places = list(itertools.product(*(range(lax.axis_size(a)) for a in across)))
    groups = [[(k + turn(*at)) % n * len(places) + i for k in range(n)] for i, at in enumerate(places)]
    return lax.all_to_all(blocks, along + across, 0, 0, axis_index_groups=groups, tiled=True)


def spread(block, along, across, turn):
    n = math.prod(lax.axis_size(a) for a in along)
    return exchange(jnp.broadcast_to(block[None], (n,) + block.shape), along, across, turn)


def by_core(c):
    return 2 * c


HBM = pl.BlockSpec(memory_space=pl.ANY)
WHOLE = pl.BlockSpec(memory_space=pltpu.VMEM)
SCALARS = pl.BlockSpec(memory_space=pltpu.SMEM)


def gather_kernel(at, tokens, t1, t3, out, sems):
    part = out.shape[2]
    own = tokens.at[:, pl.ds(pl.multiple_of(at[0] * part, part), part)]
    copies = [pltpu.make_async_copy(source, out.at[i], sems.at[i]) for i, source in enumerate((own, t1, t3))]
    for copy in copies:
        copy.start()
    for copy in copies:
        copy.wait()


def gather_tokens(at, tokens, t1, t3):
    tok, part = t1.shape
    return pl.pallas_call(
        gather_kernel,
        out_shape=jax.ShapeDtypeStruct((3, tok, part), tokens.dtype),
        in_specs=[SCALARS, HBM, HBM, HBM],
        out_specs=WHOLE,
        scratch_shapes=[pltpu.SemaphoreType.DMA((3,))],
        compiler_params=pltpu.CompilerParams(vmem_limit_bytes=16 * 2**20),
        cost_estimate=pl.CostEstimate(flops=0, bytes_accessed=2**26, transcendentals=0),
    )(at, *(pltpu.with_memory_space_constraint(p, pltpu.HBM) for p in (tokens, t1, t3)))


def load(at, core, rows_y, near, far0, far1, w, t, sem_w, sem_t):
    nl, nh, nzl = rows_y.shape[:3]
    nx, tok, width = t.shape[1:]
    half = tok // 2
    turn = by_core(at[2])
    copies = []
    for h in range(nh):
        columns = pl.ds(pl.multiple_of((2 * h + core) * width, width), width)
        places = [(near.at[i, :, columns], lax.rem(at[0] + 2 * nx - d - turn, nx), pl.ds(0, tok)) for i, d in enumerate((0, 1, 3))]
        opposite = lax.rem(at[0] + 2 * nx - 2 - turn, nx)
        places.append((far0.at[:, columns], opposite, pl.ds(0, half)))
        places.append((far1.at[:, columns], opposite, pl.ds(half, half)))
        mine = [
            pltpu.make_async_copy(source, t.at[h, block, rows], sem_t.at[h, i])
            for i, (source, block, rows) in enumerate(places)
        ]
        for l in range(nl):
            for z in range(nzl):
                place = w.at[h, :, lax.rem(z + by_core(core), nzl), lax.rem(l + core, nl)]
                mine.append(pltpu.make_async_copy(rows_y.at[l, h, z], place, sem_w.at[h, l * nzl + z]))
        for copy in mine:
            copy.start()
        copies.append(mine)
    return copies


def product(h, w, t):
    nx, tok, width = t.shape[1:]
    return jnp.dot(
        t[h].reshape(nx * tok, width), w[h].reshape(width, w.shape[-1]), preferred_element_type=jnp.float32
    )


def first_kernel(at, rows_y, near, far0, far1, total, fresh, w, t, sem_w, sem_t, sem_f):
    copies = load(at, at[2], rows_y, near, far0, far1, w, t, sem_w, sem_t)
    for h, mine in enumerate(copies):
        for copy in mine:
            copy.wait()
        total[...] = product(h, w, t) if h == 0 else total[...] + product(h, w, t)
    back = pltpu.make_async_copy(w.at[at[1]], fresh, sem_f)
    back.start()
    back.wait()


def second_kernel(at, rows_y, near, far0, far1, total, out, w, t, sem_w, sem_t, o, sem_o):
    copies = load(at, 1 - at[2], rows_y, near, far0, far1, w, t, sem_w, sem_t)
    last = len(copies) - 1
    for h, mine in enumerate(copies):
        for copy in mine:
            copy.wait()
        if h < last:
            total[...] += product(h, w, t)
        else:
            o[...] = (total[...] + product(h, w, t)).astype(o.dtype)
    back = pltpu.make_async_copy(o, out, sem_o)
    back.start()
    back.wait()


def multiply(at, rows_y, tokens, total=None):
    nl, nh, nzl, nzh, rows, kv = rows_y.shape
    nx = 4
    tok, part = tokens[0].shape[1:]
    width = part // (2 * nh)
    block = (nzh, nzl, nl, rows, kv)
    common = dict(
        compiler_params=pltpu.CompilerParams(vmem_limit_bytes=16 * 2**20),
        cost_estimate=pl.CostEstimate(
            flops=nx * tok * part * kv, bytes_accessed=4 * 2**20, transcendentals=0
        ),
    )
    scratch = [
        pltpu.VMEM((nh,) + block, jnp.bfloat16),
        pltpu.VMEM((nh, nx, tok, width), jnp.bfloat16),
        pltpu.SemaphoreType.DMA((nh, nl * nzl)),
        pltpu.SemaphoreType.DMA((nh, len(tokens) + 2)),
    ]
    if total is None:
        return pl.pallas_call(
            first_kernel,
            out_shape=(
                jax.ShapeDtypeStruct((nx * tok, kv), jnp.float32),
                jax.ShapeDtypeStruct(block, jnp.bfloat16),
            ),
            in_specs=[SCALARS] + [HBM] * 4,
            out_specs=(WHOLE, HBM),
            scratch_shapes=scratch + [pltpu.SemaphoreType.DMA],
            **common,
        )(at, rows_y, *tokens)
    return pl.pallas_call(
        second_kernel,
        out_shape=jax.ShapeDtypeStruct((nx * tok, kv), jnp.bfloat16),
        in_specs=[SCALARS] + [HBM] * 4 + [WHOLE],
        out_specs=HBM,
        scratch_shapes=scratch + [pltpu.VMEM((nx * tok, kv), jnp.bfloat16), pltpu.SemaphoreType.DMA],
        **common,
    )(at, rows_y, *tokens, total)


def local(tokens, master, momentum, trained):
    nzh, nzl, nl, nx, nh = (lax.axis_size(a) for a in ("zh", "zl", "yl", "x", "yh"))
    rows, kv = master.shape
    tok, depth = tokens.shape
    zh, zl, x, yh, c = (lax.axis_index(a) for a in ("zh", "zl", "x", "yh", "c"))
    part = depth // nx
    replicas = nzh * nzl * nl

    trained = trained[0].reshape(nzh, nzl * nl, rows, kv)
    near = lax.all_to_all(trained, ("zl", "yl"), 1, 1, tiled=True)
    near = jnp.sum(near.astype(jnp.float32), axis=1)

    start = lax.optimization_barrier(master.astype(jnp.bfloat16)).astype(jnp.float32)
    gain = outer_rate * (1 + decay_factor) / replicas
    base = master - outer_rate * ((1 + decay_factor) * start + decay_factor**2 * momentum)
    mine = (jnp.arange(nzh) == zh)[:, None, None]
    sent = jnp.where(mine, near + base / gain, near).astype(jnp.float16)
    far = spread(sent, ("zh",), ("zl", "c"), lambda zl, c: zl + 2 * c)
    fresh = (gain * jnp.sum(far.astype(jnp.float32), axis=0)).astype(jnp.bfloat16)

    near_own = lax.dynamic_index_in_dim(near, zh, 0, keepdims=False)
    others = lax.dynamic_index_in_dim(far, zh, 1, keepdims=False).astype(jnp.float32)
    from_me = (jnp.arange(nzh) == (zh + 2 * nzh - zl - 2 * c) % nzh)[:, None, None]
    summed = jnp.sum(jnp.where(from_me, near_own[None], others), axis=0)
    pseudo = start - summed / replicas
    new_momentum = decay_factor * momentum + pseudo
    new_master = master - outer_rate * (pseudo + decay_factor * new_momentum)

    at = jnp.stack([x, yh, c]).astype(jnp.int32)
    def piece(d, first=0, count=tok):
        block = lax.dynamic_slice(tokens, (first, (x + d) % nx * part), (count, part))
        return lax.ppermute(block, "x", [(i, (i + d) % nx) for i in range(nx)])

    half = tok // 2
    near_tokens = gather_tokens(at, tokens, piece(1), piece(3))
    far0, far1 = piece(2, 0, half), piece(2, half, half)
    fresh, near_tokens, far0 = lax.optimization_barrier((fresh, near_tokens, far0))

    rows_z = spread(fresh, ("zl",), ("c",), by_core)
    rows_y = spread(rows_z, ("yl", "yh"), ("c",), by_core).reshape(nl, nh, nzl, nzh, rows, kv)
    rows_y, far1, new_master, new_momentum = lax.optimization_barrier((rows_y, far1, new_master, new_momentum))
    other = lax.ppermute(rows_y, "c", [(0, 1), (1, 0)])

    far0, far1 = (pltpu.with_memory_space_constraint(p, pltpu.HBM) for p in (far0, far1))
    taken = (near_tokens, far0, far1)
    total, refreshed = multiply(at, rows_y, taken)
    share = multiply(at, other, taken, total).reshape(nx, tok, kv)
    share = exchange(share, ("x",), ("c",), by_core)
    key_values = jnp.sum(share.astype(jnp.float32), axis=0)
    return (new_master, new_momentum, refreshed.reshape(-1, kv), key_values)


def solution(mesh):
    fine = Mesh(mesh.devices.reshape(4, 4, 2, 4, 2, 2), ("zh", "zl", "yl", "x", "yh", "c"))
    replica, fsdp = ("zh", "zl", "yl"), ("x", "yh", "c")
    in_specs = (
        P(replica + fsdp, None),
        P(fsdp + replica, None),
        P(fsdp + replica, None),
        P(replica, fsdp, None),
    )
    out_specs = (
        P(fsdp + replica, None),
        P(fsdp + replica, None),
        P(fsdp, None),
        P(replica + fsdp, None),
    )
    return jax.shard_map(local, mesh=fine, in_specs=in_specs, out_specs=out_specs, check_vma=False)
```

```python
import itertools
import math

import jax
import jax.numpy as jnp
from jax import lax
from jax.experimental import pallas as pl
from jax.experimental.pallas import tpu as pltpu
from jax.sharding import Mesh, PartitionSpec as P

REPLICAS = 32
outer_rate = 0.7
decay_factor = 0.9


def exchange(blocks, along, across, turn):
    n = math.prod(lax.axis_size(a) for a in along)
    places = list(itertools.product(*(range(lax.axis_size(a)) for a in across)))
    groups = [[(k + turn(*at)) % n * len(places) + i for k in range(n)] for i, at in enumerate(places)]
    return lax.all_to_all(blocks, along + across, 0, 0, axis_index_groups=groups, tiled=True)


def exchange(blocks, along, across, turn):
    n = math.prod(lax.axis_size(a) for a in along)
    places = list(itertools.product(*(range(lax.axis_size(a)) for a in across)))
    groups = [[(k + turn(*at)) % n * len(places) + i for k in range(n)] for i, at in enumerate(places)]
    return lax.all_to_all(blocks, along + across, 0, 0, axis_index_groups=groups, tiled=True)


def exchange(blocks, along, across, turn):
    n = math.prod(lax.axis_size(a) for a in along)
    places = list(itertools.product(*(range(lax.axis_size(a)) for a in across)))
    groups = [[(k + turn(*at)) % n * len(places) + i for k in range(n)] for i, at in enumerate(places)]
    return lax.all_to_all(blocks, along + across, 0, 0, axis_index_groups=groups, tiled=True)


def exchange(blocks, along, across, turn):
    n = math.prod(lax.axis_size(a) for a in along)
    places = list(itertools.product(*(range(lax.axis_size(a)) for a in across)))
    groups = [[(k + turn(*at)) % n * len(places) + i for k in range(n)] for i, at in enumerate(places)]
    return lax.all_to_all(blocks, along + across, 0, 0, axis_index_groups=groups, tiled=True)


def exchange(blocks, along, across, turn):
    n = math.prod(lax.axis_size(a) for a in along)
    places = list(itertools.product(*(range(lax.axis_size(a)) for a in across)))
    groups = [[(k + turn(*at)) % n * len(places) + i for k in range(n)] for i, at in enumerate(places)]
    return lax.all_to_all(blocks, along + across, 0, 0, axis_index_groups=groups, tiled=True)


def exchange(blocks, along, across, turn):
    n = math.prod(lax.axis_size(a) for a in along)
    places = list(itertools.product(*(range(lax.axis_size(a)) for a in across)))
    groups = [[(k + turn(*at)) % n * len(places) + i for k in range(n)] for i, at in enumerate(places)]
    return lax.all_to_all(blocks, along + across, 0, 0, axis_index_groups=groups, tiled=True)


def exchange(blocks, along, across, turn):
    n = math.prod(lax.axis_size(a) for a in along)
    places = list(itertools.product(*(range(lax.axis_size(a)) for a in across)))
    groups = [[(k + turn(*at)) % n * len(places) + i for k in range(n)] for i, at in enumerate(places)]
    return lax.all_to_all(blocks, along + across, 0, 0, axis_index_groups=groups, tiled=True)


def exchange(blocks, along, across, turn):
    n = math.prod(lax.axis_size(a) for a in along)
    places = list(itertools.product(*(range(lax.axis_size(a)) for a in across)))
    groups = [[(k + turn(*at)) % n * len(places) + i for k in range(n)] for i, at in enumerate(places)]
    return lax.all_to_all(blocks, along + across, 0, 0, axis_index_groups=groups, tiled=True)


def exchange(blocks, along, across, turn):
    n = math.prod(lax.axis_size(a) for a in along)
    places = list(itertools.product(*(range(lax.axis_size(a)) for a in across)))
    groups = [[(k + turn(*at)) % n * len(places) + i for k in range(n)] for i, at in enumerate(places)]
    return lax.all_to_all(blocks, along + across, 0, 0, axis_index_groups=groups, tiled=True)


def exchange(blocks, along, across, turn):
    n = math.prod(lax.axis_size(a) for a in along)
    places = list(itertools.product(*(range(lax.axis_size(a)) for a in across)))
    groups = [[(k + turn(*at)) % n * len(places) + i for k in range(n)] for i, at in enumerate(places)]
    return lax.all_to_all(blocks, along + across, 0, 0, axis_index_groups=groups, tiled=True)


def exchange(blocks, along, across, turn):
    n = math.prod(lax.axis_size(a) for a in along)
    places = list(itertools.product(*(range(lax.axis_size(a)) for a in across)))
    groups = [[(k + turn(*at)) % n * len(places) + i for k in range(n)] for i, at in enumerate(places)]
    return lax.all_to_all(blocks, along + across, 0, 0, axis_index_groups=groups, tiled=True)


def exchange(blocks, along, across, turn):
    n = math.prod(lax.axis_size(a) for a in along)
    places = list(itertools.product(*(range(lax.axis_size(a)) for a in across)))
    groups = [[(k + turn(*at)) % n * len(places) + i for k in range(n)] for i, at in enumerate(places)]
    return lax.all_to_all(blocks, along + across, 0, 0, axis_index_groups=groups, tiled=True)


def exchange(blocks, along, across, turn):
    n = math.prod(lax.axis_size(a) for a in along)
    places = list(itertools.product(*(range(lax.axis_size(a)) for a in across)))
    groups = [[(k + turn(*at)) % n * len(places) + i for k in range(n)] for i, at in enumerate(places)]
    return lax.all_to_all(blocks, along + across, 0, 0, axis_index_groups=groups, tiled=True)


def exchange(blocks, along, across, turn):
    n = math.prod(lax.axis_size(a) for a in along)
    places = list(itertools.product(*(range(lax.axis_size(a)) for a in across)))
    groups = [[(k + turn(*at)) % n * len(places) + i for k in range(n)] for i, at in enumerate(places)]
    return lax.all_to_all(blocks, along + across, 0, 0, axis_index_groups=groups, tiled=True)


def spread(block, along, across, turn):
    n = math.prod(lax.axis_size(a) for a in along)
    return exchange(jnp.broadcast_to(block[None], (n,) + block.shape), along, across, turn)


def by_core(c):
    return 2 * c


HBM = pl.BlockSpec(memory_space=pl.ANY)
WHOLE = pl.BlockSpec(memory_space=pltpu.VMEM)
SCALARS = pl.BlockSpec(memory_space=pltpu.SMEM)
LIMIT = pltpu.CompilerParams(vmem_limit_bytes=16 * 2**20)
STEPS = (0, 1, 3, 2)


def gather_kernel(at, tokens, t1, t3, out, sems):
    part = out.shape[2]
    own = tokens.at[:, pl.ds(pl.multiple_of(at[0] * part, part), part)]
    copies = [
        pltpu.make_async_copy(source, out.at[i], sems.at[i]) for i, source in enumerate((own, t1, t3))
    ]
    for copy in copies:
        copy.start()
    for copy in copies:
        copy.wait()


def gather_tokens(at, tokens, t1, t3):
    tok, part = t1.shape
    return pl.pallas_call(
        gather_kernel,
        out_shape=jax.ShapeDtypeStruct((3, tok, part), tokens.dtype),
        in_specs=[SCALARS, HBM, HBM, HBM],
        out_specs=WHOLE,
        scratch_shapes=[pltpu.SemaphoreType.DMA((3,))],
        compiler_params=LIMIT,
        cost_estimate=pl.CostEstimate(flops=0, bytes_accessed=2**26, transcendentals=0),
    )(at, *(pltpu.with_memory_space_constraint(p, pltpu.HBM) for p in (tokens, t1, t3)))


def fetch(sources, places, sems):
    copies = [pltpu.make_async_copy(s, p, sems.at[i]) for i, (s, p) in enumerate(zip(sources, places))]
    for copy in copies:
        copy.start()
    return copies


def parts_of(ref, first):
    cut = first.shape[0]
    return [ref.at[pl.ds(0, cut)], ref.at[pl.ds(cut, ref.shape[0] - cut)]]


def product(core, rows_y, near, far, far_copies):
    nl, nh, nzl, nzh, rows, kv = rows_y.shape
    part = near.shape[2]
    width = part // (2 * nh)
    weights, columns = [], []
    for h in range(nh):
        weights.append(
            jnp.concatenate(
                [
                    rows_y[lax.rem(l + core, nl), h, lax.rem(z + by_core(core), nzl), zh]
                    for zh in range(nzh)
                    for z in range(nzl)
                    for l in range(nl)
                ],
                axis=0,
            )
        )
        columns.append(pl.ds(pl.multiple_of((2 * h + core) * width, width), width))
    right = jnp.concatenate(weights, axis=0)

    def times(blocks):
        left = [jnp.concatenate([block[:, cols] for block in blocks], axis=0) for cols in columns]
        return jnp.dot(jnp.concatenate(left, axis=1), right, preferred_element_type=jnp.float32)

    first = times([near.at[i] for i in range(near.shape[0])])
    for copy in far_copies:
        copy.wait()
    return jnp.concatenate([first, times([far])], axis=0), weights


def first_kernel(at, rows_y, near, far0, far1, total, fresh, w, far, sems, sem):
    copies = fetch((far0, far1), parts_of(far, far0), sems)
    result, weights = product(at[2], rows_y, near, far, copies)
    for h, block in enumerate(weights):
        w[h] = block
    back = pltpu.make_async_copy(w.at[at[1]], fresh, sem)
    back.start()
    total[...] = result
    back.wait()


def second_kernel(at, rows_y, near, far0, far1, total, out, far_here, sems):
    copies = fetch((far0, far1), parts_of(far_here, far0), sems)
    result, _ = product(1 - at[2], rows_y, near, far_here, copies)
    result = result + total[...]
    nx, tok = out.shape[:2]
    for i, step in enumerate(STEPS):
        place = lax.rem(at[0] + 2 * nx - step - by_core(at[2]), nx)
        out[place] = result[i * tok : (i + 1) * tok].astype(out.dtype)


def cost(near, kv):
    tok, part = near.shape[1:]
    return pl.CostEstimate(flops=4 * tok * part * kv, bytes_accessed=4 * 2**20, transcendentals=0)


def pinned(*arrays):
    return [pltpu.with_memory_space_constraint(a, pltpu.HBM) for a in arrays]


def first_product(at, rows_y, near, far0, far1):
    nl, nh, nzl, nzh, rows, kv = rows_y.shape
    tok, part = near.shape[1:]
    deep = nzh * nzl * nl * rows
    return pl.pallas_call(
        first_kernel,
        out_shape=(
            jax.ShapeDtypeStruct((4 * tok, kv), jnp.float32),
            jax.ShapeDtypeStruct((deep, kv), jnp.bfloat16),
        ),
        in_specs=[SCALARS, WHOLE, WHOLE, HBM, HBM],
        out_specs=(WHOLE, HBM),
        scratch_shapes=[
            pltpu.VMEM((nh, deep, kv), jnp.bfloat16),
            pltpu.VMEM((tok, part), near.dtype),
            pltpu.SemaphoreType.DMA((2,)),
            pltpu.SemaphoreType.DMA,
        ],
        compiler_params=LIMIT,
        cost_estimate=cost(near, kv),
    )(at, rows_y, near, *pinned(far0, far1))


def second_product(at, rows_y, near, far0, far1, total):
    kv = rows_y.shape[-1]
    tok, part = near.shape[1:]
    return pl.pallas_call(
        second_kernel,
        out_shape=jax.ShapeDtypeStruct((4, tok, kv), jnp.bfloat16),
        in_specs=[SCALARS, WHOLE, WHOLE, HBM, HBM, WHOLE],
        out_specs=WHOLE,
        scratch_shapes=[pltpu.VMEM((tok, part), near.dtype), pltpu.SemaphoreType.DMA((2,))],
        compiler_params=LIMIT,
        cost_estimate=cost(near, kv),
    )(at, rows_y, near, *pinned(far0, far1), total)


def local(tokens, master, momentum, trained):
    nzh, nzl, nl, nx, nh = (lax.axis_size(a) for a in ("zh", "zl", "yl", "x", "yh"))
    rows, kv = master.shape
    tok, depth = tokens.shape
    zh, x, yh, c = (lax.axis_index(a) for a in ("zh", "x", "yh", "c"))
    at = jnp.stack([x, yh, c, zh]).astype(jnp.int32)
    part = depth // nx

    trained = trained[0].reshape(nzh, nzl * nl, rows, kv)
    near = lax.all_to_all(trained, ("zl", "yl"), 1, 1, tiled=True)
    near = jnp.sum(near.astype(jnp.float32), axis=1)

    start = lax.optimization_barrier(master.astype(jnp.bfloat16))
    gain = outer_rate * (1 + decay_factor) / REPLICAS
    base = master - outer_rate * ((1 + decay_factor) * start.astype(jnp.float32) + decay_factor**2 * momentum)
    offset = base / gain
    mine = (jnp.arange(nzh) == zh)[:, None, None]
    sent = jnp.where(mine, near + offset, near).astype(jnp.float16)
    sums = spread(sent, ("zh",), ("zl", "c"), lambda zl, c: 3)
    sums = jnp.sum(sums.astype(jnp.float32), axis=0)
    fresh = (gain * sums).astype(jnp.bfloat16)

    most = tok // 2
    cuts = [lax.dynamic_slice(tokens, (0, (x + d) % nx * part), (tok, part)) for d in (1, 3, 2)]
    cuts = lax.optimization_barrier(cuts)
    cuts[2:] = lax.optimization_barrier([cuts[2][:most], cuts[2][most:]])
    t1, t3, t20, t21 = (
        lax.ppermute(cut, "x", [(i, (i + d) % nx) for i in range(nx)])
        for d, cut in ((1, cuts[0]), (3, cuts[1]), (2, cuts[2]), (2, cuts[3]))
    )
    near_tokens = gather_tokens(at, tokens, t1, t3)
    fresh, near_tokens, t20 = lax.optimization_barrier((fresh, near_tokens, t20))

    rows_z = spread(fresh, ("zl",), ("c",), by_core)
    rows_y = spread(rows_z, ("yl", "yh"), ("c",), by_core).reshape(nl, nh, nzl, nzh, rows, kv)
    summed = lax.dynamic_index_in_dim(sums, zh, 0, keepdims=False) - offset
    pseudo = start.astype(jnp.float32) - summed / REPLICAS
    new_momentum = decay_factor * momentum + pseudo
    new_master = master - outer_rate * (pseudo + decay_factor * new_momentum)
    rows_y, t21, new_master, new_momentum = lax.optimization_barrier((rows_y, t21, new_master, new_momentum))
    taken = (near_tokens, t20, t21)
    other = lax.ppermute(rows_y, "c", [(0, 1), (1, 0)])

    total, refreshed = first_product(at, rows_y, *taken)
    share = second_product(at, other, *taken, total)
    share = exchange(share, ("x",), ("c",), by_core)
    key_values = jnp.sum(share.astype(jnp.float32), axis=0)
    return (new_master, new_momentum, refreshed, key_values)


def solution(mesh):
    fine = Mesh(mesh.devices.reshape(4, 4, 2, 4, 2, 2), ("zh", "zl", "yl", "x", "yh", "c"))
    replica, fsdp = ("zh", "zl", "yl"), ("x", "yh", "c")
    in_specs = (
        P(replica + fsdp, None),
        P(fsdp + replica, None),
        P(fsdp + replica, None),
        P(replica, fsdp, None),
    )
    out_specs = (
        P(fsdp + replica, None),
        P(fsdp + replica, None),
        P(fsdp, None),
        P(replica + fsdp, None),
    )
    return jax.shard_map(local, mesh=fine, in_specs=in_specs, out_specs=out_specs, check_vma=False)
```

```python
import itertools
import math

import jax
import jax.numpy as jnp
from jax import lax
from jax.experimental import pallas as pl
from jax.experimental.pallas import tpu as pltpu
from jax.sharding import Mesh, PartitionSpec as P

REPLICAS = 32
outer_rate = 0.7
decay_factor = 0.9


def exchange(blocks, along, across, turn):
    n = math.prod(lax.axis_size(a) for a in along)
    places = list(itertools.product(*(range(lax.axis_size(a)) for a in across)))
    groups = [[(k + turn(*at)) % n * len(places) + i for k in range(n)] for i, at in enumerate(places)]
    return lax.all_to_all(blocks, along + across, 0, 0, axis_index_groups=groups, tiled=True)


def exchange(blocks, along, across, turn):
    n = math.prod(lax.axis_size(a) for a in along)
    places = list(itertools.product(*(range(lax.axis_size(a)) for a in across)))
    groups = [[(k + turn(*at)) % n * len(places) + i for k in range(n)] for i, at in enumerate(places)]
    return lax.all_to_all(blocks, along + across, 0, 0, axis_index_groups=groups, tiled=True)


def exchange(blocks, along, across, turn):
    n = math.prod(lax.axis_size(a) for a in along)
    places = list(itertools.product(*(range(lax.axis_size(a)) for a in across)))
    groups = [[(k + turn(*at)) % n * len(places) + i for k in range(n)] for i, at in enumerate(places)]
    return lax.all_to_all(blocks, along + across, 0, 0, axis_index_groups=groups, tiled=True)


def exchange(blocks, along, across, turn):
    n = math.prod(lax.axis_size(a) for a in along)
    places = list(itertools.product(*(range(lax.axis_size(a)) for a in across)))
    groups = [[(k + turn(*at)) % n * len(places) + i for k in range(n)] for i, at in enumerate(places)]
    return lax.all_to_all(blocks, along + across, 0, 0, axis_index_groups=groups, tiled=True)


def exchange(blocks, along, across, turn):
    n = math.prod(lax.axis_size(a) for a in along)
    places = list(itertools.product(*(range(lax.axis_size(a)) for a in across)))
    groups = [[(k + turn(*at)) % n * len(places) + i for k in range(n)] for i, at in enumerate(places)]
    return lax.all_to_all(blocks, along + across, 0, 0, axis_index_groups=groups, tiled=True)


def exchange(blocks, along, across, turn):
    n = math.prod(lax.axis_size(a) for a in along)
    places = list(itertools.product(*(range(lax.axis_size(a)) for a in across)))
    groups = [[(k + turn(*at)) % n * len(places) + i for k in range(n)] for i, at in enumerate(places)]
    return lax.all_to_all(blocks, along + across, 0, 0, axis_index_groups=groups, tiled=True)


def exchange(blocks, along, across, turn):
    n = math.prod(lax.axis_size(a) for a in along)
    places = list(itertools.product(*(range(lax.axis_size(a)) for a in across)))
    groups = [[(k + turn(*at)) % n * len(places) + i for k in range(n)] for i, at in enumerate(places)]
    return lax.all_to_all(blocks, along + across, 0, 0, axis_index_groups=groups, tiled=True)


def exchange(blocks, along, across, turn):
    n = math.prod(lax.axis_size(a) for a in along)
    places = list(itertools.product(*(range(lax.axis_size(a)) for a in across)))
    groups = [[(k + turn(*at)) % n * len(places) + i for k in range(n)] for i, at in enumerate(places)]
    return lax.all_to_all(blocks, along + across, 0, 0, axis_index_groups=groups, tiled=True)


def exchange(blocks, along, across, turn):
    n = math.prod(lax.axis_size(a) for a in along)
    places = list(itertools.product(*(range(lax.axis_size(a)) for a in across)))
    groups = [[(k + turn(*at)) % n * len(places) + i for k in range(n)] for i, at in enumerate(places)]
    return lax.all_to_all(blocks, along + across, 0, 0, axis_index_groups=groups, tiled=True)


def exchange(blocks, along, across, turn):
    n = math.prod(lax.axis_size(a) for a in along)
    places = list(itertools.product(*(range(lax.axis_size(a)) for a in across)))
    groups = [[(k + turn(*at)) % n * len(places) + i for k in range(n)] for i, at in enumerate(places)]
    return lax.all_to_all(blocks, along + across, 0, 0, axis_index_groups=groups, tiled=True)


def exchange(blocks, along, across, turn):
    n = math.prod(lax.axis_size(a) for a in along)
    places = list(itertools.product(*(range(lax.axis_size(a)) for a in across)))
    groups = [[(k + turn(*at)) % n * len(places) + i for k in range(n)] for i, at in enumerate(places)]
    return lax.all_to_all(blocks, along + across, 0, 0, axis_index_groups=groups, tiled=True)


def exchange(blocks, along, across, turn):
    n = math.prod(lax.axis_size(a) for a in along)
    places = list(itertools.product(*(range(lax.axis_size(a)) for a in across)))
    groups = [[(k + turn(*at)) % n * len(places) + i for k in range(n)] for i, at in enumerate(places)]
    return lax.all_to_all(blocks, along + across, 0, 0, axis_index_groups=groups, tiled=True)


def exchange(blocks, along, across, turn):
    n = math.prod(lax.axis_size(a) for a in along)
    places = list(itertools.product(*(range(lax.axis_size(a)) for a in across)))
    groups = [[(k + turn(*at)) % n * len(places) + i for k in range(n)] for i, at in enumerate(places)]
    return lax.all_to_all(blocks, along + across, 0, 0, axis_index_groups=groups, tiled=True)


def exchange(blocks, along, across, turn):
    n = math.prod(lax.axis_size(a) for a in along)
    places = list(itertools.product(*(range(lax.axis_size(a)) for a in across)))
    groups = [[(k + turn(*at)) % n * len(places) + i for k in range(n)] for i, at in enumerate(places)]
    return lax.all_to_all(blocks, along + across, 0, 0, axis_index_groups=groups, tiled=True)


def exchange(blocks, along, across, turn):
    n = math.prod(lax.axis_size(a) for a in along)
    places = list(itertools.product(*(range(lax.axis_size(a)) for a in across)))
    groups = [[(k + turn(*at)) % n * len(places) + i for k in range(n)] for i, at in enumerate(places)]
    return lax.all_to_all(blocks, along + across, 0, 0, axis_index_groups=groups, tiled=True)


def exchange(blocks, along, across, turn):
    n = math.prod(lax.axis_size(a) for a in along)
    places = list(itertools.product(*(range(lax.axis_size(a)) for a in across)))
    groups = [[(k + turn(*at)) % n * len(places) + i for k in range(n)] for i, at in enumerate(places)]
    return lax.all_to_all(blocks, along + across, 0, 0, axis_index_groups=groups, tiled=True)


def exchange(blocks, along, across, turn):
    n = math.prod(lax.axis_size(a) for a in along)
    places = list(itertools.product(*(range(lax.axis_size(a)) for a in across)))
    groups = [[(k + turn(*at)) % n * len(places) + i for k in range(n)] for i, at in enumerate(places)]
    return lax.all_to_all(blocks, along + across, 0, 0, axis_index_groups=groups, tiled=True)


def exchange(blocks, along, across, turn):
    n = math.prod(lax.axis_size(a) for a in along)
    places = list(itertools.product(*(range(lax.axis_size(a)) for a in across)))
    groups = [[(k + turn(*at)) % n * len(places) + i for k in range(n)] for i, at in enumerate(places)]
    return lax.all_to_all(blocks, along + across, 0, 0, axis_index_groups=groups, tiled=True)


def exchange(blocks, along, across, turn):
    n = math.prod(lax.axis_size(a) for a in along)
    places = list(itertools.product(*(range(lax.axis_size(a)) for a in across)))
    groups = [[(k + turn(*at)) % n * len(places) + i for k in range(n)] for i, at in enumerate(places)]
    return lax.all_to_all(blocks, along + across, 0, 0, axis_index_groups=groups, tiled=True)


def exchange(blocks, along, across, turn):
    n = math.prod(lax.axis_size(a) for a in along)
    places = list(itertools.product(*(range(lax.axis_size(a)) for a in across)))
    groups = [[(k + turn(*at)) % n * len(places) + i for k in range(n)] for i, at in enumerate(places)]
    return lax.all_to_all(blocks, along + across, 0, 0, axis_index_groups=groups, tiled=True)


def exchange(blocks, along, across, turn):
    n = math.prod(lax.axis_size(a) for a in along)
    places = list(itertools.product(*(range(lax.axis_size(a)) for a in across)))
    groups = [[(k + turn(*at)) % n * len(places) + i for k in range(n)] for i, at in enumerate(places)]
    return lax.all_to_all(blocks, along + across, 0, 0, axis_index_groups=groups, tiled=True)


def spread(block, along, across, turn):
    n = math.prod(lax.axis_size(a) for a in along)
    return exchange(jnp.broadcast_to(block[None], (n,) + block.shape), along, across, turn)


def by_core(c):
    return 2 * c


HBM = pl.BlockSpec(memory_space=pl.ANY)
WHOLE = pl.BlockSpec(memory_space=pltpu.VMEM)
SCALARS = pl.BlockSpec(memory_space=pltpu.SMEM)
LIMIT = pltpu.CompilerParams(vmem_limit_bytes=16 * 2**20)
STEPS = (0, 1, 3, 2)


def gather_kernel(at, tokens, t1, t3, out, sems):
    part = out.shape[2]
    own = tokens.at[:, pl.ds(pl.multiple_of(at[0] * part, part), part)]
    copies = [pltpu.make_async_copy(source, out.at[i], sems.at[i]) for i, source in enumerate((own, t1, t3))]
    for copy in copies:
        copy.start()
    for copy in copies:
        copy.wait()


def join_kernel(first, second, out, sems):
    cut = first.shape[0]
    places = (out.at[pl.ds(0, cut)], out.at[pl.ds(cut, out.shape[0] - cut)])
    copies = [pltpu.make_async_copy(s, p, sems.at[i]) for i, (s, p) in enumerate(zip((first, second), places))]
    for copy in copies:
        copy.start()
    for copy in copies:
        copy.wait()


def pinned(*arrays):
    return [pltpu.with_memory_space_constraint(a, pltpu.HBM) for a in arrays]


def moved(shape, copies):
    return dict(
        out_shape=jax.ShapeDtypeStruct(shape, jnp.bfloat16),
        out_specs=WHOLE,
        scratch_shapes=[pltpu.SemaphoreType.DMA((copies,))],
        compiler_params=LIMIT,
        cost_estimate=pl.CostEstimate(flops=2**34, bytes_accessed=2**26, transcendentals=0),
    )


def gather_tokens(at, tokens, t1, t3):
    specs = [SCALARS, HBM, HBM, HBM]
    return pl.pallas_call(gather_kernel, in_specs=specs, **moved((3,) + t1.shape, 3))(at, *pinned(tokens, t1, t3))


def join_tokens(first, second):
    shape = (first.shape[0] + second.shape[0], first.shape[1])
    return pl.pallas_call(join_kernel, in_specs=[HBM, HBM], **moved(shape, 2))(*pinned(first, second))


def product(core, rows_y, near, far):
    nl, nh, nzl, nzh, rows, kv = rows_y.shape
    part = near.shape[2]
    width = part // (2 * nh)
    weights, columns = [], []
    for h in range(nh):
        weights.append(
            jnp.concatenate(
                [
                    rows_y[lax.rem(l + core, nl), h, lax.rem(z + by_core(core), nzl), zh]
                    for zh in range(nzh)
                    for z in range(nzl)
                    for l in range(nl)
                ],
                axis=0,
            )
        )
        columns.append(pl.ds(pl.multiple_of((2 * h + core) * width, width), width))
    right = jnp.concatenate(weights, axis=0)
    blocks = [near.at[i] for i in range(near.shape[0])] + [far]
    left = [jnp.concatenate([block[:, cols] for block in blocks], axis=0) for cols in columns]
    return jnp.dot(jnp.concatenate(left, axis=1), right, preferred_element_type=jnp.float32), weights


def first_kernel(at, rows_y, near, far, total, fresh, w, sem):
    result, weights = product(at[2], rows_y, near, far)
    for h, block in enumerate(weights):
        w[h] = block
    back = pltpu.make_async_copy(w.at[at[1]], fresh, sem)
    back.start()
    total[...] = result
    back.wait()


def second_kernel(at, rows_y, near, far, total, out):
    result, _ = product(1 - at[2], rows_y, near, far)
    result = result + total[...]
    nx, tok = out.shape[:2]
    for i, step in enumerate(STEPS):
        place = lax.rem(at[0] + 2 * nx - step - by_core(at[2]), nx)
        out[place] = result[i * tok : (i + 1) * tok].astype(out.dtype)


def cost(near, kv):
    tok, part = near.shape[1:]
    return pl.CostEstimate(flops=4 * tok * part * kv, bytes_accessed=4 * 2**20, transcendentals=0)


def first_product(at, rows_y, near, far):
    nl, nh, nzl, nzh, rows, kv = rows_y.shape
    tok = far.shape[0]
    deep = nzh * nzl * nl * rows
    return pl.pallas_call(
        first_kernel,
        out_shape=(
            jax.ShapeDtypeStruct((4 * tok, kv), jnp.float32),
            jax.ShapeDtypeStruct((deep, kv), jnp.bfloat16),
        ),
        in_specs=[SCALARS, WHOLE, WHOLE, WHOLE],
        out_specs=(WHOLE, HBM),
        scratch_shapes=[pltpu.VMEM((nh, deep, kv), jnp.bfloat16), pltpu.SemaphoreType.DMA],
        compiler_params=LIMIT,
        cost_estimate=cost(near, kv),
    )(at, rows_y, near, far)


def second_product(at, rows_y, near, far, total):
    kv = rows_y.shape[-1]
    return pl.pallas_call(
        second_kernel,
        out_shape=jax.ShapeDtypeStruct((4, far.shape[0], kv), jnp.bfloat16),
        in_specs=[SCALARS, WHOLE, WHOLE, WHOLE, WHOLE],
        out_specs=WHOLE,
        compiler_params=LIMIT,
        cost_estimate=cost(near, kv),
    )(at, rows_y, near, far, total)


def local(tokens, master, momentum, trained):
    nzh, nzl, nl, nx, nh = (lax.axis_size(a) for a in ("zh", "zl", "yl", "x", "yh"))
    rows, kv = master.shape
    tok, depth = tokens.shape
    zh, x, yh, c = (lax.axis_index(a) for a in ("zh", "x", "yh", "c"))
    at = jnp.stack([x, yh, c, zh]).astype(jnp.int32)
    part = depth // nx

    trained = trained[0].reshape(nzh, nzl * nl, rows, kv)
    near = lax.all_to_all(trained, ("zl", "yl"), 1, 1, tiled=True)
    near = jnp.sum(near.astype(jnp.float32), axis=1)

    start = lax.optimization_barrier(master.astype(jnp.bfloat16))
    gain = outer_rate * (1 + decay_factor) / REPLICAS
    base = master - outer_rate * ((1 + decay_factor) * start.astype(jnp.float32) + decay_factor**2 * momentum)
    offset = base / gain
    mine = (jnp.arange(nzh) == zh)[:, None, None]
    sent = jnp.where(mine, near + offset, near).astype(jnp.float16)
    sums = spread(sent, ("zh",), ("zl", "c"), lambda zl, c: 2)
    sums = jnp.sum(sums.astype(jnp.float32), axis=0)
    fresh = (gain * sums).astype(jnp.bfloat16)

    most = tok // 2
    cuts = [lax.dynamic_slice(tokens, (0, (x + d) % nx * part), (tok, part)) for d in (1, 3, 2)]
    cuts = lax.optimization_barrier(cuts)
    cuts[2:] = lax.optimization_barrier([cuts[2][:most], cuts[2][most:]])
    t1, t3, t20, t21 = (
        lax.ppermute(cut, "x", [(i, (i + d) % nx) for i in range(nx)])
        for d, cut in ((1, cuts[0]), (3, cuts[1]), (2, cuts[2]), (2, cuts[3]))
    )
    near_tokens = gather_tokens(at, tokens, t1, t3)
    fresh, near_tokens, t20 = lax.optimization_barrier((fresh, near_tokens, t20))

    rows_z = spread(fresh, ("zl",), ("c",), by_core)
    rows_y = spread(rows_z, ("yl", "yh"), ("c",), by_core).reshape(nl, nh, nzl, nzh, rows, kv)
    summed = lax.dynamic_index_in_dim(sums, zh, 0, keepdims=False) - offset
    pseudo = start.astype(jnp.float32) - summed / REPLICAS
    new_momentum = decay_factor * momentum + pseudo
    new_master = master - outer_rate * (pseudo + decay_factor * new_momentum)
    rows_y, new_master, new_momentum = lax.optimization_barrier((rows_y, new_master, new_momentum))
    taken = (near_tokens, join_tokens(t20, t21))
    other = lax.ppermute(rows_y, "c", [(0, 1), (1, 0)])

    total, refreshed = first_product(at, rows_y, *taken)
    share = second_product(at, other, *taken, total)
    share = exchange(share, ("x",), ("c",), by_core)
    key_values = jnp.sum(share.astype(jnp.float32), axis=0)
    return (new_master, new_momentum, refreshed, key_values)


def solution(mesh):
    fine = Mesh(mesh.devices.reshape(4, 4, 2, 4, 2, 2), ("zh", "zl", "yl", "x", "yh", "c"))
    replica, fsdp = ("zh", "zl", "yl"), ("x", "yh", "c")
    in_specs = (
        P(replica + fsdp, None),
        P(fsdp + replica, None),
        P(fsdp + replica, None),
        P(replica, fsdp, None),
    )
    out_specs = (
        P(fsdp + replica, None),
        P(fsdp + replica, None),
        P(fsdp, None),
        P(replica + fsdp, None),
    )
    return jax.shard_map(local, mesh=fine, in_specs=in_specs, out_specs=out_specs, check_vma=False)
```

```python
import itertools
import math

import jax
import jax.numpy as jnp
from jax import lax
from jax.experimental import pallas as pl
from jax.experimental.pallas import tpu as pltpu
from jax.sharding import Mesh, PartitionSpec as P

REPLICAS = 32
outer_rate = 0.7
decay_factor = 0.9


def exchange(blocks, along, across, turn):
    n = math.prod(lax.axis_size(a) for a in along)
    places = list(itertools.product(*(range(lax.axis_size(a)) for a in across)))
    groups = [[(k + turn(*at)) % n * len(places) + i for k in range(n)] for i, at in enumerate(places)]
    return lax.all_to_all(blocks, along + across, 0, 0, axis_index_groups=groups, tiled=True)


def exchange(blocks, along, across, turn):
    n = math.prod(lax.axis_size(a) for a in along)
    places = list(itertools.product(*(range(lax.axis_size(a)) for a in across)))
    groups = [[(k + turn(*at)) % n * len(places) + i for k in range(n)] for i, at in enumerate(places)]
    return lax.all_to_all(blocks, along + across, 0, 0, axis_index_groups=groups, tiled=True)


def exchange(blocks, along, across, turn):
    n = math.prod(lax.axis_size(a) for a in along)
    places = list(itertools.product(*(range(lax.axis_size(a)) for a in across)))
    groups = [[(k + turn(*at)) % n * len(places) + i for k in range(n)] for i, at in enumerate(places)]
    return lax.all_to_all(blocks, along + across, 0, 0, axis_index_groups=groups, tiled=True)


def exchange(blocks, along, across, turn):
    n = math.prod(lax.axis_size(a) for a in along)
    places = list(itertools.product(*(range(lax.axis_size(a)) for a in across)))
    groups = [[(k + turn(*at)) % n * len(places) + i for k in range(n)] for i, at in enumerate(places)]
    return lax.all_to_all(blocks, along + across, 0, 0, axis_index_groups=groups, tiled=True)


def exchange(blocks, along, across, turn):
    n = math.prod(lax.axis_size(a) for a in along)
    places = list(itertools.product(*(range(lax.axis_size(a)) for a in across)))
    groups = [[(k + turn(*at)) % n * len(places) + i for k in range(n)] for i, at in enumerate(places)]
    return lax.all_to_all(blocks, along + across, 0, 0, axis_index_groups=groups, tiled=True)


def exchange(blocks, along, across, turn):
    n = math.prod(lax.axis_size(a) for a in along)
    places = list(itertools.product(*(range(lax.axis_size(a)) for a in across)))
    groups = [[(k + turn(*at)) % n * len(places) + i for k in range(n)] for i, at in enumerate(places)]
    return lax.all_to_all(blocks, along + across, 0, 0, axis_index_groups=groups, tiled=True)


def exchange(blocks, along, across, turn):
    n = math.prod(lax.axis_size(a) for a in along)
    places = list(itertools.product(*(range(lax.axis_size(a)) for a in across)))
    groups = [[(k + turn(*at)) % n * len(places) + i for k in range(n)] for i, at in enumerate(places)]
    return lax.all_to_all(blocks, along + across, 0, 0, axis_index_groups=groups, tiled=True)


def exchange(blocks, along, across, turn):
    n = math.prod(lax.axis_size(a) for a in along)
    places = list(itertools.product(*(range(lax.axis_size(a)) for a in across)))
    groups = [[(k + turn(*at)) % n * len(places) + i for k in range(n)] for i, at in enumerate(places)]
    return lax.all_to_all(blocks, along + across, 0, 0, axis_index_groups=groups, tiled=True)


def exchange(blocks, along, across, turn):
    n = math.prod(lax.axis_size(a) for a in along)
    places = list(itertools.product(*(range(lax.axis_size(a)) for a in across)))
    groups = [[(k + turn(*at)) % n * len(places) + i for k in range(n)] for i, at in enumerate(places)]
    return lax.all_to_all(blocks, along + across, 0, 0, axis_index_groups=groups, tiled=True)


def exchange(blocks, along, across, turn):
    n = math.prod(lax.axis_size(a) for a in along)
    places = list(itertools.product(*(range(lax.axis_size(a)) for a in across)))
    groups = [[(k + turn(*at)) % n * len(places) + i for k in range(n)] for i, at in enumerate(places)]
    return lax.all_to_all(blocks, along + across, 0, 0, axis_index_groups=groups, tiled=True)


def exchange(blocks, along, across, turn):
    n = math.prod(lax.axis_size(a) for a in along)
    places = list(itertools.product(*(range(lax.axis_size(a)) for a in across)))
    groups = [[(k + turn(*at)) % n * len(places) + i for k in range(n)] for i, at in enumerate(places)]
    return lax.all_to_all(blocks, along + across, 0, 0, axis_index_groups=groups, tiled=True)


def exchange(blocks, along, across, turn):
    n = math.prod(lax.axis_size(a) for a in along)
    places = list(itertools.product(*(range(lax.axis_size(a)) for a in across)))
    groups = [[(k + turn(*at)) % n * len(places) + i for k in range(n)] for i, at in enumerate(places)]
    return lax.all_to_all(blocks, along + across, 0, 0, axis_index_groups=groups, tiled=True)


def exchange(blocks, along, across, turn):
    n = math.prod(lax.axis_size(a) for a in along)
    places = list(itertools.product(*(range(lax.axis_size(a)) for a in across)))
    groups = [[(k + turn(*at)) % n * len(places) + i for k in range(n)] for i, at in enumerate(places)]
    return lax.all_to_all(blocks, along + across, 0, 0, axis_index_groups=groups, tiled=True)


def exchange(blocks, along, across, turn):
    n = math.prod(lax.axis_size(a) for a in along)
    places = list(itertools.product(*(range(lax.axis_size(a)) for a in across)))
    groups = [[(k + turn(*at)) % n * len(places) + i for k in range(n)] for i, at in enumerate(places)]
    return lax.all_to_all(blocks, along + across, 0, 0, axis_index_groups=groups, tiled=True)


def exchange(blocks, along, across, turn):
    n = math.prod(lax.axis_size(a) for a in along)
    places = list(itertools.product(*(range(lax.axis_size(a)) for a in across)))
    groups = [[(k + turn(*at)) % n * len(places) + i for k in range(n)] for i, at in enumerate(places)]
    return lax.all_to_all(blocks, along + across, 0, 0, axis_index_groups=groups, tiled=True)


def exchange(blocks, along, across, turn):
    n = math.prod(lax.axis_size(a) for a in along)
    places = list(itertools.product(*(range(lax.axis_size(a)) for a in across)))
    groups = [[(k + turn(*at)) % n * len(places) + i for k in range(n)] for i, at in enumerate(places)]
    return lax.all_to_all(blocks, along + across, 0, 0, axis_index_groups=groups, tiled=True)


def exchange(blocks, along, across, turn):
    n = math.prod(lax.axis_size(a) for a in along)
    places = list(itertools.product(*(range(lax.axis_size(a)) for a in across)))
    groups = [[(k + turn(*at)) % n * len(places) + i for k in range(n)] for i, at in enumerate(places)]
    return lax.all_to_all(blocks, along + across, 0, 0, axis_index_groups=groups, tiled=True)


def exchange(blocks, along, across, turn):
    n = math.prod(lax.axis_size(a) for a in along)
    places = list(itertools.product(*(range(lax.axis_size(a)) for a in across)))
    groups = [[(k + turn(*at)) % n * len(places) + i for k in range(n)] for i, at in enumerate(places)]
    return lax.all_to_all(blocks, along + across, 0, 0, axis_index_groups=groups, tiled=True)


def exchange(blocks, along, across, turn):
    n = math.prod(lax.axis_size(a) for a in along)
    places = list(itertools.product(*(range(lax.axis_size(a)) for a in across)))
    groups = [[(k + turn(*at)) % n * len(places) + i for k in range(n)] for i, at in enumerate(places)]
    return lax.all_to_all(blocks, along + across, 0, 0, axis_index_groups=groups, tiled=True)


def exchange(blocks, along, across, turn):
    n = math.prod(lax.axis_size(a) for a in along)
    places = list(itertools.product(*(range(lax.axis_size(a)) for a in across)))
    groups = [[(k + turn(*at)) % n * len(places) + i for k in range(n)] for i, at in enumerate(places)]
    return lax.all_to_all(blocks, along + across, 0, 0, axis_index_groups=groups, tiled=True)


def exchange(blocks, along, across, turn):
    n = math.prod(lax.axis_size(a) for a in along)
    places = list(itertools.product(*(range(lax.axis_size(a)) for a in across)))
    groups = [[(k + turn(*at)) % n * len(places) + i for k in range(n)] for i, at in enumerate(places)]
    return lax.all_to_all(blocks, along + across, 0, 0, axis_index_groups=groups, tiled=True)


def exchange(blocks, along, across, turn):
    n = math.prod(lax.axis_size(a) for a in along)
    places = list(itertools.product(*(range(lax.axis_size(a)) for a in across)))
    groups = [[(k + turn(*at)) % n * len(places) + i for k in range(n)] for i, at in enumerate(places)]
    return lax.all_to_all(blocks, along + across, 0, 0, axis_index_groups=groups, tiled=True)


def spread(block, along, across, turn):
    n = math.prod(lax.axis_size(a) for a in along)
    return exchange(jnp.broadcast_to(block[None], (n,) + block.shape), along, across, turn)


def by_core(c):
    return 2 * c


HBM = pl.BlockSpec(memory_space=pl.ANY)
WHOLE = pl.BlockSpec(memory_space=pltpu.VMEM)
SCALARS = pl.BlockSpec(memory_space=pltpu.SMEM)
LIMIT = pltpu.CompilerParams(vmem_limit_bytes=16 * 2**20)
STEPS = (0, 1, 3, 2)


def gather_kernel(at, tokens, t1, t3, out, sems):
    part = out.shape[2]
    own = tokens.at[:, pl.ds(pl.multiple_of(at[0] * part, part), part)]
    copies = [pltpu.make_async_copy(source, out.at[i], sems.at[i]) for i, source in enumerate((own, t1, t3))]
    for copy in copies:
        copy.start()
    for copy in copies:
        copy.wait()


def join_kernel(first, second, out, sems):
    cut = first.shape[0]
    places = (out.at[pl.ds(0, cut)], out.at[pl.ds(cut, out.shape[0] - cut)])
    copies = [pltpu.make_async_copy(s, p, sems.at[i]) for i, (s, p) in enumerate(zip((first, second), places))]
    for copy in copies:
        copy.start()
    for copy in copies:
        copy.wait()


def pinned(*arrays):
    return [pltpu.with_memory_space_constraint(a, pltpu.HBM) for a in arrays]


def moved(shape, copies):
    return dict(
        out_shape=jax.ShapeDtypeStruct(shape, jnp.bfloat16),
        out_specs=WHOLE,
        scratch_shapes=[pltpu.SemaphoreType.DMA((copies,))],
        compiler_params=LIMIT,
        cost_estimate=pl.CostEstimate(flops=2**34, bytes_accessed=2**26, transcendentals=0),
    )


def gather_tokens(at, tokens, t1, t3):
    specs = [SCALARS, HBM, HBM, HBM]
    return pl.pallas_call(gather_kernel, in_specs=specs, **moved((3,) + t1.shape, 3))(at, *pinned(tokens, t1, t3))


def join_tokens(first, second):
    shape = (first.shape[0] + second.shape[0], first.shape[1])
    return pl.pallas_call(join_kernel, in_specs=[HBM, HBM], **moved(shape, 2))(*pinned(first, second))


def product(core, rows_y, near, far):
    nl, nh, nzl, nzh, rows, kv = rows_y.shape
    part = near.shape[2]
    width = part // (2 * nh)
    weights, columns = [], []
    for h in range(nh):
        weights.append(
            jnp.concatenate(
                [
                    rows_y[lax.rem(l + core, nl), h, lax.rem(z + by_core(core), nzl), zh]
                    for zh in range(nzh)
                    for z in range(nzl)
                    for l in range(nl)
                ],
                axis=0,
            )
        )
        columns.append(pl.ds(pl.multiple_of((2 * h + core) * width, width), width))
    right = jnp.concatenate(weights, axis=0)
    blocks = [near.at[i] for i in range(near.shape[0])] + [far]
    left = [jnp.concatenate([block[:, cols] for block in blocks], axis=0) for cols in columns]
    return jnp.dot(jnp.concatenate(left, axis=1), right, preferred_element_type=jnp.float32), weights


def first_kernel(at, rows_y, near, far, total, fresh, w, sem):
    result, weights = product(at[2], rows_y, near, far)
    for h, block in enumerate(weights):
        w[h] = block
    back = pltpu.make_async_copy(w.at[at[1]], fresh, sem)
    back.start()
    total[...] = result
    back.wait()


def second_kernel(at, rows_y, near, far, total, out):
    result, _ = product(1 - at[2], rows_y, near, far)
    result = result + total[...]
    nx, tok = out.shape[:2]
    for i, step in enumerate(STEPS):
        place = lax.rem(at[0] + 2 * nx - step - by_core(at[2]), nx)
        out[place] = result[i * tok : (i + 1) * tok].astype(out.dtype)


def cost(near, kv):
    tok, part = near.shape[1:]
    return pl.CostEstimate(flops=4 * tok * part * kv, bytes_accessed=4 * 2**20, transcendentals=0)


def first_product(at, rows_y, near, far):
    nl, nh, nzl, nzh, rows, kv = rows_y.shape
    tok = far.shape[0]
    deep = nzh * nzl * nl * rows
    return pl.pallas_call(
        first_kernel,
        out_shape=(
            jax.ShapeDtypeStruct((4 * tok, kv), jnp.float32),
            jax.ShapeDtypeStruct((deep, kv), jnp.bfloat16),
        ),
        in_specs=[SCALARS, WHOLE, WHOLE, WHOLE],
        out_specs=(WHOLE, HBM),
        scratch_shapes=[pltpu.VMEM((nh, deep, kv), jnp.bfloat16), pltpu.SemaphoreType.DMA],
        compiler_params=LIMIT,
        cost_estimate=cost(near, kv),
    )(at, rows_y, near, far)


def second_product(at, rows_y, near, far, total):
    kv = rows_y.shape[-1]
    return pl.pallas_call(
        second_kernel,
        out_shape=jax.ShapeDtypeStruct((4, far.shape[0], kv), jnp.bfloat16),
        in_specs=[SCALARS, WHOLE, WHOLE, WHOLE, WHOLE],
        out_specs=WHOLE,
        compiler_params=LIMIT,
        cost_estimate=cost(near, kv),
    )(at, rows_y, near, far, total)


def local(tokens, master, momentum, trained):
    nzh, nzl, nl, nx, nh = (lax.axis_size(a) for a in ("zh", "zl", "yl", "x", "yh"))
    rows, kv = master.shape
    tok, depth = tokens.shape
    zh, x, yh, c = (lax.axis_index(a) for a in ("zh", "x", "yh", "c"))
    at = jnp.stack([x, yh, c, zh]).astype(jnp.int32)
    part = depth // nx

    trained = trained[0].reshape(nzh, nzl * nl, rows, kv)
    near = lax.all_to_all(trained, ("zl", "yl"), 1, 1, tiled=True)
    near = jnp.sum(near.astype(jnp.float32), axis=1)

    start = lax.optimization_barrier(master.astype(jnp.bfloat16))
    gain = outer_rate * (1 + decay_factor) / REPLICAS
    base = master - outer_rate * ((1 + decay_factor) * start.astype(jnp.float32) + decay_factor**2 * momentum)
    offset = base / gain
    mine = (jnp.arange(nzh) == zh)[:, None, None]
    sent = jnp.where(mine, near + offset, near).astype(jnp.float16)
    sums = spread(sent, ("zh",), ("zl", "c"), lambda zl, c: 2)
    sums = jnp.sum(sums.astype(jnp.float32), axis=0)
    fresh = (gain * sums).astype(jnp.bfloat16)

    most = tok * 2 // 3
    cuts = [lax.dynamic_slice(tokens, (0, (x + d) % nx * part), (tok, part)) for d in (1, 3, 2)]
    cuts = lax.optimization_barrier(cuts)
    cuts[2:] = lax.optimization_barrier([cuts[2][:most], cuts[2][most:]])
    t1, t3, t20, t21 = (
        lax.ppermute(cut, "x", [(i, (i + d) % nx) for i in range(nx)])
        for d, cut in ((1, cuts[0]), (3, cuts[1]), (2, cuts[2]), (2, cuts[3]))
    )
    near_tokens = gather_tokens(at, tokens, t1, t3)
    fresh, near_tokens, t20 = lax.optimization_barrier((fresh, near_tokens, t20))

    rows_z = spread(fresh, ("zl",), ("c",), by_core)
    rows_y = spread(rows_z, ("yl", "yh"), ("c",), by_core).reshape(nl, nh, nzl, nzh, rows, kv)
    summed = lax.dynamic_index_in_dim(sums, zh, 0, keepdims=False) - offset
    pseudo = start.astype(jnp.float32) - summed / REPLICAS
    new_momentum = decay_factor * momentum + pseudo
    new_master = master - outer_rate * (pseudo + decay_factor * new_momentum)
    rows_y, new_master, new_momentum = lax.optimization_barrier((rows_y, new_master, new_momentum))
    taken = (near_tokens, join_tokens(t20, t21))
    other = lax.ppermute(rows_y, "c", [(0, 1), (1, 0)])

    total, refreshed = first_product(at, rows_y, *taken)
    share = second_product(at, other, *taken, total)
    share = exchange(share, ("x",), ("c",), by_core)
    key_values = jnp.sum(share.astype(jnp.float32), axis=0)
    return (new_master, new_momentum, refreshed, key_values)


def solution(mesh):
    fine = Mesh(mesh.devices.reshape(4, 4, 2, 4, 2, 2), ("zh", "zl", "yl", "x", "yh", "c"))
    replica, fsdp = ("zh", "zl", "yl"), ("x", "yh", "c")
    in_specs = (
        P(replica + fsdp, None),
        P(fsdp + replica, None),
        P(fsdp + replica, None),
        P(replica, fsdp, None),
    )
    out_specs = (
        P(fsdp + replica, None),
        P(fsdp + replica, None),
        P(fsdp, None),
        P(replica + fsdp, None),
    )
    return jax.shard_map(local, mesh=fine, in_specs=in_specs, out_specs=out_specs, check_vma=False)
```

```python
import itertools
import math

import jax
import jax.numpy as jnp
from jax import lax
from jax.experimental import pallas as pl
from jax.experimental.pallas import tpu as pltpu
from jax.sharding import Mesh, PartitionSpec as P

REPLICAS = 32
outer_rate = 0.7
decay_factor = 0.9


def exchange(blocks, along, across, turn):
    n = math.prod(lax.axis_size(a) for a in along)
    places = list(itertools.product(*(range(lax.axis_size(a)) for a in across)))
    groups = [[(k + turn(*at)) % n * len(places) + i for k in range(n)] for i, at in enumerate(places)]
    return lax.all_to_all(blocks, along + across, 0, 0, axis_index_groups=groups, tiled=True)


def spread(block, along, across, turn):
    n = math.prod(lax.axis_size(a) for a in along)
    return exchange(jnp.broadcast_to(block[None], (n,) + block.shape), along, across, turn)


def by_core(c):
    return 2 * c


HBM = pl.BlockSpec(memory_space=pl.ANY)
WHOLE = pl.BlockSpec(memory_space=pltpu.VMEM)
SCALARS = pl.BlockSpec(memory_space=pltpu.SMEM)
LIMIT = pltpu.CompilerParams(vmem_limit_bytes=16 * 2**20)
STEPS = (0, 1, 3, 2)


def gather_kernel(at, tokens, t1, t3, out, sems):
    part = out.shape[2]
    own = tokens.at[:, pl.ds(pl.multiple_of(at[0] * part, part), part)]
    copies = [pltpu.make_async_copy(source, out.at[i], sems.at[i]) for i, source in enumerate((own, t1, t3))]
    for copy in copies:
        copy.start()
    for copy in copies:
        copy.wait()


def join_kernel(first, second, out, sems):
    cut = first.shape[0]
    places = (out.at[pl.ds(0, cut)], out.at[pl.ds(cut, out.shape[0] - cut)])
    copies = [pltpu.make_async_copy(s, p, sems.at[i]) for i, (s, p) in enumerate(zip((first, second), places))]
    for copy in copies:
        copy.start()
    for copy in copies:
        copy.wait()


def pinned(*arrays):
    return [pltpu.with_memory_space_constraint(a, pltpu.HBM) for a in arrays]


def moved(shape, copies):
    return dict(
        out_shape=jax.ShapeDtypeStruct(shape, jnp.bfloat16),
        out_specs=WHOLE,
        scratch_shapes=[pltpu.SemaphoreType.DMA((copies,))],
        compiler_params=LIMIT,
        cost_estimate=pl.CostEstimate(flops=2**34, bytes_accessed=2**26, transcendentals=0),
    )


def gather_tokens(at, tokens, t1, t3):
    specs = [SCALARS, HBM, HBM, HBM]
    return pl.pallas_call(gather_kernel, in_specs=specs, **moved((3,) + t1.shape, 3))(at, *pinned(tokens, t1, t3))


def join_tokens(first, second):
    shape = (first.shape[0] + second.shape[0], first.shape[1])
    return pl.pallas_call(join_kernel, in_specs=[HBM, HBM], **moved(shape, 2))(*pinned(first, second))


def product(core, rows_y, near, far):
    nl, nh, nzl, nzh, rows, kv = rows_y.shape
    part = near.shape[2]
    width = part // (2 * nh)
    weights, columns = [], []
    for h in range(nh):
        weights.append(
            jnp.concatenate(
                [
                    rows_y[lax.rem(l + core, nl), h, lax.rem(z + by_core(core), nzl), zh]
                    for zh in range(nzh)
                    for z in range(nzl)
                    for l in range(nl)
                ],
                axis=0,
            )
        )
        columns.append(pl.ds(pl.multiple_of((2 * h + core) * width, width), width))
    right = jnp.concatenate(weights, axis=0)
    blocks = [near.at[i] for i in range(near.shape[0])] + [far]
    left = [jnp.concatenate([block[:, cols] for block in blocks], axis=0) for cols in columns]
    return jnp.dot(jnp.concatenate(left, axis=1), right, preferred_element_type=jnp.float32), weights


def first_kernel(at, rows_y, near, far, total, fresh, w, sem):
    result, weights = product(at[2], rows_y, near, far)
    for h, block in enumerate(weights):
        w[h] = block
    back = pltpu.make_async_copy(w.at[at[1]], fresh, sem)
    back.start()
    total[...] = result
    back.wait()


def second_kernel(at, rows_y, near, far, total, out):
    result, _ = product(1 - at[2], rows_y, near, far)
    result = result + total[...]
    nx, tok = out.shape[:2]
    for i, step in enumerate(STEPS):
        place = lax.rem(at[0] + 2 * nx - step - by_core(at[2]), nx)
        out[place] = result[i * tok : (i + 1) * tok].astype(out.dtype)


def cost(near, kv):
    tok, part = near.shape[1:]
    return pl.CostEstimate(flops=4 * tok * part * kv, bytes_accessed=4 * 2**20, transcendentals=0)


def first_product(at, rows_y, near, far):
    nl, nh, nzl, nzh, rows, kv = rows_y.shape
    tok = far.shape[0]
    deep = nzh * nzl * nl * rows
    return pl.pallas_call(
        first_kernel,
        out_shape=(
            jax.ShapeDtypeStruct((4 * tok, kv), jnp.float32),
            jax.ShapeDtypeStruct((deep, kv), jnp.bfloat16),
        ),
        in_specs=[SCALARS, WHOLE, WHOLE, WHOLE],
        out_specs=(WHOLE, HBM),
        scratch_shapes=[pltpu.VMEM((nh, deep, kv), jnp.bfloat16), pltpu.SemaphoreType.DMA],
        compiler_params=LIMIT,
        cost_estimate=cost(near, kv),
    )(at, rows_y, near, far)


def second_product(at, rows_y, near, far, total):
    kv = rows_y.shape[-1]
    return pl.pallas_call(
        second_kernel,
        out_shape=jax.ShapeDtypeStruct((4, far.shape[0], kv), jnp.bfloat16),
        in_specs=[SCALARS, WHOLE, WHOLE, WHOLE, WHOLE],
        out_specs=WHOLE,
        compiler_params=LIMIT,
        cost_estimate=cost(near, kv),
    )(at, rows_y, near, far, total)


def local(tokens, master, momentum, trained):
    nzh, nzl, nl, nx, nh = (lax.axis_size(a) for a in ("zh", "zl", "yl", "x", "yh"))
    rows, kv = master.shape
    tok, depth = tokens.shape
    zh, x, yh, c = (lax.axis_index(a) for a in ("zh", "x", "yh", "c"))
    at = jnp.stack([x, yh, c, zh]).astype(jnp.int32)
    part = depth // nx

    trained = trained[0].reshape(nzh, nzl * nl, rows, kv)
    near = lax.all_to_all(trained, ("zl", "yl"), 1, 1, tiled=True)
    near = jnp.sum(near.astype(jnp.float32), axis=1)

    start = lax.optimization_barrier(master.astype(jnp.bfloat16))
    gain = outer_rate * (1 + decay_factor) / REPLICAS
    base = master - outer_rate * ((1 + decay_factor) * start.astype(jnp.float32) + decay_factor**2 * momentum)
    offset = base / gain
    mine = (jnp.arange(nzh) == zh)[:, None, None]
    sent = jnp.where(mine, near + offset, near).astype(jnp.float16)
    sums = spread(sent, ("zh",), ("zl", "c"), lambda zl, c: 2)
    sums = jnp.sum(sums.astype(jnp.float32), axis=0)
    fresh = (gain * sums).astype(jnp.bfloat16)

    most = tok * 2 // 3
    cuts = [lax.dynamic_slice(tokens, (0, (x + d) % nx * part), (tok, part)) for d in (1, 3, 2)]
    cuts = lax.optimization_barrier(cuts)
    cuts[2:] = lax.optimization_barrier([cuts[2][:most], cuts[2][most:]])
    t1, t3, t20, t21 = (
        lax.ppermute(cut, "x", [(i, (i + d) % nx) for i in range(nx)])
        for d, cut in ((1, cuts[0]), (3, cuts[1]), (2, cuts[2]), (2, cuts[3]))
    )
    near_tokens = gather_tokens(at, tokens, t1, t3)
    fresh, near_tokens, t20 = lax.optimization_barrier((fresh, near_tokens, t20))

    rows_z = spread(fresh, ("zl",), ("c",), by_core)
    rows_y = spread(rows_z, ("yl", "yh"), ("c",), by_core).reshape(nl, nh, nzl, nzh, rows, kv)
    summed = lax.dynamic_index_in_dim(sums, zh, 0, keepdims=False) - offset
    pseudo = start.astype(jnp.float32) - summed / REPLICAS
    new_momentum = decay_factor * momentum + pseudo
    new_master = master - outer_rate * (pseudo + decay_factor * new_momentum)
    rows_y, new_master, new_momentum = lax.optimization_barrier((rows_y, new_master, new_momentum))
    taken = (near_tokens, join_tokens(t20, t21))
    other = lax.ppermute(rows_y, "c", [(0, 1), (1, 0)])

    total, refreshed = first_product(at, rows_y, *taken)
    share = second_product(at, other, *taken, total)
    share = exchange(share, ("x",), ("c",), by_core)
    key_values = jnp.sum(share.astype(jnp.float32), axis=0)
    return (new_master, new_momentum, refreshed, key_values)


def solution(mesh):
    fine = Mesh(mesh.devices.reshape(4, 4, 2, 4, 2, 2), ("zh", "zl", "yl", "x", "yh", "c"))
    replica, fsdp = ("zh", "zl", "yl"), ("x", "yh", "c")
    in_specs = (
        P(replica + fsdp, None),
        P(fsdp + replica, None),
        P(fsdp + replica, None),
        P(replica, fsdp, None),
    )
    out_specs = (
        P(fsdp + replica, None),
        P(fsdp + replica, None),
        P(fsdp, None),
        P(replica + fsdp, None),
    )
    return jax.shard_map(local, mesh=fine, in_specs=in_specs, out_specs=out_specs, check_vma=False)
```
